32 devices in a mesh: dp: 4 (over z), ctx: 2 (over y), tp: 4 (over x, core).
Axes of the slice: x: 2, y: 2, z: 4, core: 2. Of those that a mesh axis runs over, the one named last changes fastest.
Arguments:
- tokens: bfloat16 [8, 2048, 1024], P('dp', 'ctx'), may hold values from -6 to 6
- lengths: int32 [8, 4], P('dp'), may hold values from 1 to 1025, 2048 in all within a row
- w_q: bfloat16 [1024, 1024], P(('dp', 'ctx'), 'tp'), may hold values from -0.1875 to 0.1875
- w_k: bfloat16 [1024, 1024], P(('dp', 'ctx'), 'tp'), may hold values from -0.1875 to 0.1875
- w_v: bfloat16 [1024, 2048], P(('dp', 'ctx'), 'tp'), may hold values from -0.1875 to 0.1875
- w_g: bfloat16 [1024, 2048], P(('dp', 'ctx'), 'tp'), may hold values from -0.1875 to 0.1875
- w_a: bfloat16 [1024, 8], P(('dp', 'ctx'), 'tp'), may hold values from -0.1875 to 0.1875
- w_b: bfloat16 [1024, 8], P(('dp', 'ctx'), 'tp'), may hold values from -0.1875 to 0.1875
- output_weight: bfloat16 [1024, 2048], P(('dp', 'ctx'), 'tp'), may hold values from -0.1875 to 0.1875
- w_gate: bfloat16 [1024, 2816], P(('dp', 'ctx'), 'tp'), may hold values from -0.1875 to 0.1875
- w_up: bfloat16 [1024, 2816], P(('dp', 'ctx'), 'tp'), may hold values from -0.1875 to 0.1875
- w_down: bfloat16 [1024, 2816], P(('dp', 'ctx'), 'tp'), may hold values from -0.15625 to 0.15625
- gain_attn: bfloat16 [1024], P(('dp', 'ctx')), may hold values from 0.5 to 1.5
- gain_ffn: bfloat16 [1024], P(('dp', 'ctx')), may hold values from 0.5 to 1.5
- gain_out: bfloat16 [256], P(('dp', 'ctx')), may hold values from 0.5 to 1.5
- conv_q: bfloat16 [4, 1024], P(None, 'tp'), may hold values from -3 to 3
- conv_k: bfloat16 [4, 1024], P(None, 'tp'), may hold values from -3 to 3
- conv_v: bfloat16 [4, 2048], P(None, 'tp'), may hold values from -3 to 3
- a_log: float32 [8], P('tp'), may hold values from 0 to 2.7
- dt_bias: float32 [8], P('tp'), may hold values from -8 to -3
- d_out: bfloat16 [8, 2048, 1024], P('dp', 'ctx'), may hold values from -6 to 6
Outputs:
- layer_out: bfloat16 [8, 2048, 1024], P('dp', 'ctx')
- grad_tokens: float32 [8, 2048, 1024], P('dp', 'ctx')
- grad_w_q: float32 [1024, 1024], P(('dp', 'ctx'), 'tp')
- grad_w_k: float32 [1024, 1024], P(('dp', 'ctx'), 'tp')
- grad_w_v: float32 [1024, 2048], P(('dp', 'ctx'), 'tp')
- grad_w_g: float32 [1024, 2048], P(('dp', 'ctx'), 'tp')
- grad_w_a: float32 [1024, 8], P(('dp', 'ctx'), 'tp')
- grad_w_b: float32 [1024, 8], P(('dp', 'ctx'), 'tp')
- grad_w_o: float32 [1024, 2048], P(('dp', 'ctx'), 'tp')
- grad_w_gate: float32 [1024, 2816], P(('dp', 'ctx'), 'tp')
- grad_w_up: float32 [1024, 2816], P(('dp', 'ctx'), 'tp')
- grad_w_down: float32 [1024, 2816], P(('dp', 'ctx'), 'tp')
- grad_gain_attn: float32 [1024], P(('dp', 'ctx'))
- grad_gain_ffn: float32 [1024], P(('dp', 'ctx'))
- grad_gain_out: float32 [256], P(('dp', 'ctx'))
- grad_conv_q: float32 [4, 1024], P(None, 'tp')
- grad_conv_k: float32 [4, 1024], P(None, 'tp')
- grad_conv_v: float32 [4, 2048], P(None, 'tp')
- grad_a_log: float32 [8], P('tp')
- grad_dt_bias: float32 [8], P('tp')
The draws below stay inside these ranges and needn't reach their ends.
Inputs may be any that keep to these rules, and one draw needn't show every extreme that they name: In each stream the 4 lengths sum to 2048, and one of them is exactly 1025.
All inputs are finite; a program needn't handle non-finite values.
Results may differ from the reference program's by a relative error of at most 0.014.
Values may be sent and summed in bfloat16 or wider, within the bound.
A program may use at most 320 MiB of HBM per device.

```python
import math
import jax
import jax.numpy as jnp
import numpy as np
from jax import lax

D = 1024
H = 8
DV = 256
FF = 2816
CONV = 4
BLOCK = 64
NSEQ = 4
HK = 1024
HV = 2048
BATCH = 8
STREAM = 2048
MOST = 1025


def steps_of(rng, shape, shards, least, high):
    def one(position, parts):
        heights = jax.random.uniform(jax.random.fold_in(jax.random.fold_in(rng, 6), position), (parts,), jnp.float32, least / len(shards), high / len(shards))
        return jnp.repeat(jnp.exp(heights), shape[position] // parts).reshape((-1,) + (1,) * (len(shape) - position - 1))

    level = one(*shards[0])
    for cut in shards[1:]:
        level = level * one(*cut)
    return level


def profile(count, total, bound, slope):
    portions = [(1 << 20) // math.isqrt(grade ** slope) + 1 for grade in range(2, count + 1)]
    spare, counts = total - bound - (count - 1), [1] * (count - 1)
    while spare > 0:
        movable = [i for i in range(count - 1) if counts[i] < bound]
        whole, left = sum([portions[i] for i in movable]), spare
        for i in movable:
            extra = min(bound - counts[i], max(1, left * portions[i] // whole), spare)
            counts[i] = counts[i] + extra
            spare = spare - extra
    return np.array([bound] + counts)


def ragged(stream_key, count, total, limit, skew):
    if count == 2:
        one = jax.random.randint(stream_key, (), max(1, total - limit), min(limit, total - 1) + 1)
        return jnp.stack([one, total - one])
    sizes = jnp.asarray(profile(count, total, limit, skew), jnp.int32)
    couples = (count - 1) // 2
    giver, receiver = sizes[1:1 + 2 * couples:2], sizes[2:2 + 2 * couples:2]
    room = jnp.minimum(giver - 1, limit - receiver)
    moved = jax.random.randint(jax.random.fold_in(stream_key, 1), (couples,), 0, 1 << 20) % (room + 1)
    sizes = sizes.at[1:1 + 2 * couples:2].set(giver - moved).at[2:2 + 2 * couples:2].set(receiver + moved)
    return sizes[jax.random.permutation(jax.random.fold_in(stream_key, 2), count)]


def scatter_about(stream_key, shape, width, bound, cuts=(), kind=jnp.bfloat16):
    level = steps_of(stream_key, shape, cuts, -0.22, 0.18) if cuts else 1.0
    values = jax.random.normal(stream_key, shape, jnp.float32) * width * level
    return jnp.minimum(jnp.maximum(values, -bound), bound).astype(kind)


def setup_inputs(seed: int = 0) -> dict:
    key_list = jax.random.split(jax.random.key(seed), 22)
    return {
        "tokens": scatter_about(key_list[0], (BATCH, STREAM, D), 1.0, 6.0, ((0, 4), (1, 2))),
        "lengths": jax.vmap(lambda own: ragged(own, NSEQ, STREAM, MOST, 2))(jax.random.split(key_list[1], BATCH)).reshape((BATCH, NSEQ)).astype(jnp.int32),
        "w_q": scatter_about(key_list[2], (D, HK), D ** -0.5, 0.1875, ((0, 8), (1, 4))),
        "w_k": scatter_about(key_list[3], (D, HK), D ** -0.5, 0.1875, ((0, 8), (1, 4))),
        "w_v": scatter_about(key_list[4], (D, HV), D ** -0.5, 0.1875, ((0, 8), (1, 4))),
        "w_g": scatter_about(key_list[5], (D, HV), D ** -0.5, 0.1875, ((0, 8), (1, 4))),
        "w_a": scatter_about(key_list[6], (D, H), D ** -0.5, 0.1875, ((0, 8), (1, 4))),
        "w_b": scatter_about(key_list[7], (D, H), D ** -0.5, 0.1875, ((0, 8), (1, 4))),
        "output_weight": scatter_about(key_list[8], (D, HV), (HV // 2) ** -0.5, 0.1875, ((0, 8), (1, 4))),
        "w_gate": scatter_about(key_list[9], (D, FF), D ** -0.5, 0.1875, ((0, 8), (1, 4))),
        "w_up": scatter_about(key_list[10], (D, FF), D ** -0.5, 0.1875, ((0, 8), (1, 4))),
        "w_down": scatter_about(key_list[11], (D, FF), (FF // 2) ** -0.5, 0.15625, ((0, 8), (1, 4))),
        "gain_attn": jnp.clip(1.0 + 0.1 * jax.random.normal(key_list[12], (D,), jnp.float32), 0.5, 1.5).astype(jnp.bfloat16),
        "gain_ffn": jnp.clip(1.0 + 0.1 * jax.random.normal(key_list[13], (D,), jnp.float32), 0.5, 1.5).astype(jnp.bfloat16),
        "gain_out": jnp.clip(1.0 + 0.1 * jax.random.normal(key_list[14], (DV,), jnp.float32), 0.5, 1.5).astype(jnp.bfloat16),
        "conv_q": scatter_about(key_list[15], (CONV, HK), CONV ** -0.5, 3.0, ((1, 4),)),
        "conv_k": scatter_about(key_list[16], (CONV, HK), CONV ** -0.5, 3.0, ((1, 4),)),
        "conv_v": scatter_about(key_list[17], (CONV, HV), CONV ** -0.5, 3.0, ((1, 4),)),
        "a_log": jnp.clip(2.7 * jax.random.uniform(key_list[18], (H,), jnp.float32) ** steps_of(key_list[18], (H,), ((0, 4),), -0.2, 0.2), 0.0, 2.7),
        "dt_bias": jnp.clip(-8.0 + 5.0 * jax.random.uniform(key_list[19], (H,), jnp.float32) ** steps_of(key_list[19], (H,), ((0, 4),), -0.2, 0.2), -8.0, -3.0),
        "d_out": scatter_about(key_list[20], (BATCH, STREAM, D), 1.0, 6.0, ((0, 4), (1, 2))),
    }


highest_precision = lax.Precision.HIGHEST
norm_epsilon = 1e-05
unit_epsilon = 1e-06

@jax.custom_vjp
def lower_precision(v):
    return lax.optimization_barrier(v.astype(jnp.bfloat16)).astype(jnp.float32)

@jax.custom_vjp
def lower_precision_backward(v):
    return v

def low_keep(v):
    return (lower_precision(v), None)

def low_pass(kept, grad):
    return (grad,)

def back_keep(v):
    return (v, None)

def back_low(kept, grad):
    return (lower_precision(grad),)
lower_precision.defvjp(low_keep, low_pass)
lower_precision_backward.defvjp(back_keep, back_low)

def norm_gain(values, gain):
    return values * lax.rsqrt(lax.optimization_barrier(jnp.mean(values * values, -1, keepdims=True)) + norm_epsilon) * gain

def project(left_operand, weight_matrix):
    return jnp.einsum('nxq,qz->nxz', left_operand, weight_matrix, precision=highest_precision)

def make_masks(lengths, seq_len, conv_width):
    halo_rows = conv_width - 1
    positions = jnp.arange(seq_len + halo_rows, dtype=jnp.int32) - halo_rows
    seq_ends = jnp.cumsum(lengths, axis=-1)
    segment = lax.optimization_barrier(jnp.sum((seq_ends[:, None, :] <= positions[None, :, None]).astype(jnp.int32), -1))
    own_segment = segment[:, halo_rows:]
    tap_masks = [((segment[:, offset:offset + seq_len] == own_segment) & (positions[offset:offset + seq_len] >= 0)[None, :]).astype(jnp.float32) for offset in range(conv_width)]
    keep_mask = ((own_segment == segment[:, halo_rows - 1:halo_rows - 1 + seq_len]) & (positions[halo_rows:] > 0)[None, :]).astype(jnp.float32)
    return (tap_masks, keep_mask)

def causal_conv(raw_cols, weight_matrix, tap_masks):
    conv_width = weight_matrix.shape[0]
    seq_len = raw_cols.shape[1]
    padded = jnp.pad(raw_cols, ((0, 0), (conv_width - 1, 0), (0, 0)))
    summed = padded[:, 0:seq_len] * weight_matrix[0] * tap_masks[0][..., None]
    for offset in range(1, conv_width):
        summed = summed + padded[:, offset:offset + seq_len] * weight_matrix[offset] * tap_masks[offset][..., None]
    return summed

def token_step(memory, inputs):
    queries, key_rows, values, decays, beta_gate = inputs
    decayed = decays[..., None, None] * memory
    predicted = jnp.einsum('ghvd,ghd->ghv', decayed, key_rows, precision=highest_precision)
    memory = decayed + jnp.einsum('ghv,ghd->ghvd', beta_gate[..., None] * (values - predicted), key_rows, precision=highest_precision)
    return (memory, jnp.einsum('ghvd,ghd->ghv', memory, queries, precision=highest_precision))

def run_span(memory, inputs):
    return lax.scan(token_step, memory, inputs)

def recurrence(queries, key_rows, values, decays, beta_gate):
    groups, seq_len, head_count, key_dim = queries.shape
    val_dim = values.shape[-1]
    block_count = seq_len // BLOCK

    def arrange(tensor):
        shifted = jnp.moveaxis(tensor, 1, 0)
        return shifted.reshape((block_count, BLOCK) + shifted.shape[1:])
    memory = jnp.zeros((groups, head_count, val_dim, key_dim), jnp.float32)
    memory, outputs = lax.scan(jax.checkpoint(run_span), memory, (arrange(queries), arrange(key_rows), arrange(values), arrange(decays), arrange(beta_gate)))
    outputs = outputs.reshape((seq_len,) + outputs.shape[2:])
    return jnp.moveaxis(outputs, 0, 1)

def layer_block(weights, stream_x, stream_lengths):
    w_q, w_k, w_v, w_g, w_a, w_b, output_weight, w_gate, w_up, w_down, gain_attn, gain_ffn, gain_out, conv_q, conv_k, conv_v, a_log, dt_bias = weights
    groups, seq_len = (stream_x.shape[0], stream_x.shape[1])
    head_count = a_log.shape[0]
    key_dim = w_q.shape[1] // head_count
    val_dim = w_v.shape[1] // head_count
    tap_masks, keep_mask = make_masks(stream_lengths, seq_len, conv_q.shape[0])
    normed = lower_precision(norm_gain(stream_x, gain_attn))
    q_raw = lower_precision_backward(lower_precision(project(normed, w_q)))
    k_raw = lower_precision_backward(lower_precision(project(normed, w_k)))
    v_raw = lower_precision_backward(lower_precision(project(normed, w_v)))
    g_raw = lower_precision_backward(project(normed, w_g))
    a_raw = lower_precision_backward(project(normed, w_a))
    b_raw = lower_precision_backward(project(normed, w_b))
    queries = jax.nn.silu(causal_conv(q_raw, conv_q, tap_masks)).reshape(groups, seq_len, head_count, key_dim)
    key_rows = jax.nn.silu(causal_conv(k_raw, conv_k, tap_masks)).reshape(groups, seq_len, head_count, key_dim)
    values = jax.nn.silu(causal_conv(v_raw, conv_v, tap_masks)).reshape(groups, seq_len, head_count, val_dim)
    queries = queries * lax.rsqrt(lax.optimization_barrier(jnp.sum(queries * queries, -1, keepdims=True)) + unit_epsilon) * key_dim ** (-0.5)
    key_rows = key_rows * lax.rsqrt(lax.optimization_barrier(jnp.sum(key_rows * key_rows, -1, keepdims=True)) + unit_epsilon)
    log_decay = -jnp.exp(a_log) * jax.nn.softplus(a_raw + dt_bias)
    decays = keep_mask[..., None] * jnp.exp(log_decay)
    beta_gate = jax.nn.sigmoid(b_raw)
    direct = recurrence(queries, key_rows, values, decays, beta_gate)
    scaled = direct * lax.rsqrt(lax.optimization_barrier(jnp.mean(direct * direct, -1, keepdims=True)) + norm_epsilon) * gain_out
    gated_output = (scaled * jax.nn.silu(g_raw.reshape(groups, seq_len, head_count, val_dim))).reshape(groups, seq_len, head_count * val_dim)
    attention_result = lower_precision_backward(jnp.einsum('yex,tx->yet', lower_precision(gated_output), output_weight, precision=highest_precision))
    middle = stream_x + attention_result
    normed_ffn = lower_precision(norm_gain(middle, gain_ffn))
    gate_val = lower_precision_backward(project(normed_ffn, w_gate))
    up_val = lower_precision_backward(project(normed_ffn, w_up))
    hidden = lower_precision(jax.nn.silu(gate_val) * up_val)
    return middle + jnp.einsum('glf,df->gld', hidden, w_down, precision=highest_precision)

def reference(tokens, lengths, w_q, w_k, w_v, w_g, w_a, w_b, output_weight, w_gate, w_up, w_down, gain_attn, gain_ffn, gain_out, conv_q, conv_k, conv_v, a_log, dt_bias, d_out):
    weights = tuple((tensor.astype(jnp.float32) for tensor in (w_q, w_k, w_v, w_g, w_a, w_b, output_weight, w_gate, w_up, w_down, gain_attn, gain_ffn, gain_out, conv_q, conv_k, conv_v, a_log, dt_bias)))
    batch_rows, seq_len, model_width = tokens.shape
    group_size = 2
    group_count = batch_rows // group_size
    grouped_len = lengths.reshape(group_count, group_size, lengths.shape[-1])
    rematted = jax.checkpoint(layer_block)

    def forward(stream_x, weight_set):
        grouped = stream_x.reshape(group_count, group_size, seq_len, model_width)

        def scan_step(unused, inputs):
            return (unused, rematted(weight_set, inputs[0], inputs[1]))
        unused, outputs = lax.scan(scan_step, jnp.zeros((), jnp.float32), (grouped, grouped_len))
        return outputs.reshape(batch_rows, seq_len, model_width)
    result, pullback = jax.vjp(forward, tokens.astype(jnp.float32), weights)
    d_tokens, d_weights = pullback(d_out.astype(jnp.float32))
    return (result.astype(jnp.bfloat16), d_tokens, d_weights[0], d_weights[1], d_weights[2], d_weights[3], d_weights[4], d_weights[5], d_weights[6], d_weights[7], d_weights[8], d_weights[9], d_weights[10], d_weights[11], d_weights[12], d_weights[13], d_weights[14], d_weights[15], d_weights[16], d_weights[17])
```

```python
from functools import partial

import jax
import jax.numpy as jnp
from jax import lax
from jax.sharding import PartitionSpec as P

BLOCK = 64


highest_precision = lax.Precision.HIGHEST
norm_epsilon = 1e-05
unit_epsilon = 1e-06
PRECISION = lax.Precision.HIGH


def from_behind(value, axis, steps):
    count = lax.axis_size(axis)
    leading, last = (max(0, -steps), min(count, count - steps))
    return lax.ppermute(value, axis, [(source, source + steps) for source in range(leading, last)])


def state_entering(last, val_dim, axis):
    count, here = (lax.axis_size(axis), lax.axis_index(axis))
    if count == 2:
        return from_behind(last[:, :, :val_dim], axis, 1)
    everything = lax.all_gather(last, axis)
    state = everything[0][:, :, :val_dim]
    state = jnp.where(here > 0, state, 0.0)
    for k in range(1, count - 1):
        new = (
            jnp.einsum(
                "bhij,bhjk->bhik", state, everything[k][:, :, val_dim:], precision=highest_precision
            )
            + everything[k][:, :, :val_dim]
        )
        state = jnp.where(k < here, new, state)
    return state


def gradient_entering(first, val_dim, axis):
    count, here = (lax.axis_size(axis), lax.axis_index(axis))
    low = first.astype(jnp.bfloat16)
    if count == 2:
        return from_behind(low[:, :, :val_dim], axis, -1).astype(jnp.float32)
    everything = lax.all_gather(low, axis).astype(jnp.float32)
    state = jnp.where(here < count - 1, everything[count - 1][:, :, :val_dim], 0.0)
    for k in range(count - 2, 0, -1):
        new = (
            jnp.einsum(
                "bhij,bhjk->bhik", state, everything[k][:, :, val_dim:], precision=highest_precision
            )
            + everything[k][:, :, :val_dim]
        )
        state = jnp.where(k > here, new, state)
    return state


def sum_over_tp(part):
    count, here = (lax.axis_size("tp"), lax.axis_index("tp"))
    low = part.astype(jnp.bfloat16)
    if count != 4:
        return lax.psum(low, "tp")
    half = part.shape[0] // 2
    even = lax.rem(here, 2) == 0
    near = [(i, i ^ 1) for i in range(count)]
    far = [(i, i ^ 2) for i in range(count)]
    keep = jnp.where(even, low[:half], low[half:])
    send = jnp.where(even, low[half:], low[:half])
    received = lax.ppermute(send, "tp", near)
    pair = (keep.astype(jnp.float32) + received.astype(jnp.float32)).astype(jnp.bfloat16)
    other = lax.ppermute(pair, "tp", far)
    total = (pair.astype(jnp.float32) + other.astype(jnp.float32)).astype(jnp.bfloat16)
    peer = lax.ppermute(total, "tp", near)
    return jnp.concatenate([jnp.where(even, total, peer), jnp.where(even, peer, total)], 0)


def summed_product(left, right, spec):
    return jnp.stack(
        [
            sum_over_tp(jnp.einsum(spec, left[b], right, preferred_element_type=jnp.float32))
            for b in range(left.shape[0])
        ]
    )


def norm_gain(values, gain):
    return values * lax.rsqrt(jnp.mean(values * values, -1, keepdims=True) + norm_epsilon) * gain


def segment_ids(positions, lengths):
    seq_ends = jnp.cumsum(lengths, axis=-1)
    return jnp.sum((seq_ends[:, None, :] <= positions[None, :, None]).astype(jnp.int32), -1)


def mm(spec, left, right):
    return jnp.einsum(spec, left, right, precision=PRECISION)


@jax.custom_vjp
def unit_lower_inverse(coupling):
    size = coupling.shape[-1]
    row = jnp.arange(size)[:, None]
    col = jnp.arange(size)[None, :]

    def off(width):
        return (
            (row // (2 * width) == col // (2 * width))
            & (row // width % 2 == 1)
            & (col // width % 2 == 0)
        )

    inverse = jnp.eye(size, dtype=jnp.float32) - jnp.where(off(1), coupling, 0.0)
    width = 2
    while width < size:
        piece = jnp.where(off(width), coupling, 0.0)
        inverse = inverse - mm(
            "nbhij,nbhjk->nbhik", mm("nbhij,nbhjk->nbhik", inverse, piece), inverse
        )
        width *= 2
    return inverse


def inverse_keep(coupling):
    inverse = unit_lower_inverse(coupling)
    return inverse, inverse


def inverse_back(inverse, grad):
    inner = mm("nbhji,nbhjk->nbhik", inverse, grad)
    return (-mm("nbhij,nbhkj->nbhik", inner, inverse),)


unit_lower_inverse.defvjp(inverse_keep, inverse_back)


def arrange(tensor):
    streams, seg_len = tensor.shape[:2]
    shaped = tensor.reshape((streams, seg_len // BLOCK, BLOCK) + tensor.shape[2:])
    return shaped.transpose((1, 0, 3, 2, 4) if tensor.ndim == 4 else (1, 0, 3, 2))


def arrange_back(tensor):
    blocks, streams, head_count, _, width = tensor.shape
    return tensor.transpose(1, 0, 3, 2, 4).reshape(streams, blocks * BLOCK, head_count, width)


def block_maps(queries, key_rows, values, log_decay, beta_gate, resets):
    q, k, v = arrange(queries), arrange(key_rows), arrange(values)
    d, b = arrange(log_decay), arrange(beta_gate)
    z = jnp.cumsum(arrange(resets[..., None]), -1)
    row = jnp.arange(BLOCK)[:, None]
    col = jnp.arange(BLOCK)[None, :]
    summed = jnp.einsum(
        "nbhs,ts->nbht", d, (row >= col).astype(jnp.float32), precision=highest_precision
    )
    inside = (z[..., :, None] == z[..., None, :]) & (row >= col)
    ratio = jnp.where(
        inside,
        jnp.exp(jnp.where(inside, summed[..., :, None] - summed[..., None, :], 0.0)),
        0.0,
    )
    from_start = jnp.where(z == 0, jnp.exp(summed), 0.0)
    gram = mm("nbhtd,nbhsd->nbhts", k, k)
    coupling = jnp.where(row > col, b[..., None] * ratio * gram, 0.0)
    inverse = unit_lower_inverse(coupling)
    wrote = mm("nbhts,nbhsv->nbhtv", inverse, b[..., None] * v)
    erased = mm("nbhts,nbhsd->nbhtd", inverse, (b * from_start)[..., None] * k)
    scores = ratio * mm("nbhtd,nbhsd->nbhts", q, k)
    offset = mm("nbhts,nbhsv->nbhtv", scores, wrote)
    reader = from_start[..., None] * q - mm("nbhts,nbhsd->nbhtd", scores, erased)
    late_keys = ratio[..., BLOCK - 1, :, None] * k
    eye = jnp.eye(k.shape[-1], dtype=jnp.float32)
    moved = from_start[..., BLOCK - 1, None, None] * eye - mm(
        "nbhtd,nbhte->nbhde", erased, late_keys
    )
    added = mm("nbhtv,nbhtd->nbhvd", wrote, late_keys)
    return moved, added, reader, offset


def run_blocks(moves, adds, spec, order):
    blocks, streams, heads, rows, width = adds.shape
    eye = jnp.broadcast_to(jnp.eye(width, dtype=jnp.float32), (streams, heads, width, width))
    memory = jnp.concatenate([jnp.zeros((streams, heads, rows, width), jnp.float32), eye], 2)
    padded = jnp.pad(adds, ((0, 0), (0, 0), (0, 0), (0, width), (0, 0)))
    states = [None] * blocks
    for n in order:
        states[n] = memory
        memory = mm(spec, memory, moves[n]) + padded[n]
    return jnp.stack(states), memory


def finish(direct, gate_raw, gain_out):
    streams, seg_len, head_count, val_dim = direct.shape
    scaled = (
        direct * lax.rsqrt(jnp.mean(direct * direct, -1, keepdims=True) + norm_epsilon) * gain_out
    )
    gated_output = scaled * jax.nn.silu(gate_raw.reshape(streams, seg_len, head_count, val_dim))
    return gated_output.reshape(streams, seg_len, head_count * val_dim)


def on_device(
    tokens,
    lengths,
    w_q,
    w_k,
    w_v,
    w_g,
    w_a,
    w_b,
    output_weight,
    w_gate,
    w_up,
    w_down,
    gain_attn,
    gain_ffn,
    gain_out,
    conv_q,
    conv_k,
    conv_v,
    a_log,
    dt_bias,
    d_out,
):
    shards = ("dp", "ctx")
    shard_count = lax.axis_size(shards)
    shard_rows = w_q.shape[0]
    gain_rows = gain_out.shape[0]
    first_pack = jnp.concatenate(
        [
            w_q,
            w_k,
            w_v,
            w_g,
            w_a,
            w_b,
            gain_attn[:, None],
            gain_ffn[:, None],
            jnp.pad(gain_out, (0, shard_rows - gain_rows))[:, None],
        ],
        1,
    )
    w_first = lax.all_gather(first_pack, shards, axis=0, tiled=True)
    second_pack = jnp.concatenate([output_weight, w_gate, w_up, w_down], 1)
    second_pack, w_first = lax.optimization_barrier((second_pack, w_first))
    w_second = lax.all_gather(second_pack, shards, axis=0, tiled=True)
    streams, seg_len = (tokens.shape[0], tokens.shape[1])
    head_count = a_log.shape[0]
    key_cols = w_q.shape[1]
    val_cols = w_v.shape[1]
    key_dim = key_cols // head_count
    val_dim = val_cols // head_count
    hidden_cols = w_gate.shape[1]
    conv_width = conv_q.shape[0]
    mixed_cols = 2 * key_cols + val_cols
    halo_rows = conv_width - 1
    positions = (
        lax.axis_index("ctx") * seg_len
        - halo_rows
        + jnp.arange(seg_len + halo_rows, dtype=jnp.int32)
    )
    segment = segment_ids(positions, lengths)
    own_segment = segment[:, halo_rows:]
    tap_masks = [
        (
            (segment[:, offset : offset + seg_len] == own_segment)
            & (positions[offset : offset + seg_len] >= 0)[None, :]
        ).astype(jnp.float32)[..., None]
        for offset in range(conv_width)
    ]
    keep_mask = (own_segment == segment[:, halo_rows - 1 : halo_rows - 1 + seg_len]) & (
        positions[halo_rows:] > 0
    )[None, :]
    resets = 1 - keep_mask.astype(jnp.int32)
    tokens_f = tokens.astype(jnp.float32)
    main_cols = mixed_cols + val_cols
    side_cols_all = 2 * head_count
    gains = w_first[:, main_cols + side_cols_all :].astype(jnp.float32)
    gain_attn_f = gains[:, 0]
    gain_ffn_f = gains[:, 1]
    gain_out_f = gains[:, 2].reshape(shard_count, shard_rows)[:, :gain_rows].reshape(-1)
    w_main = w_first[:, :main_cols]
    w_side = w_first[:, main_cols : main_cols + side_cols_all]
    w_o = w_second[:, :val_cols]
    w_pair = w_second[:, val_cols : val_cols + 2 * hidden_cols]
    w_back = w_second[:, val_cols + 2 * hidden_cols :]
    normed = norm_gain(tokens_f, gain_attn_f).astype(jnp.bfloat16)
    projected = jnp.einsum("bsd,dc->bsc", normed, w_main, preferred_element_type=jnp.float32)
    mixed_raw = projected[..., :mixed_cols].astype(jnp.bfloat16)
    gate_raw = projected[..., mixed_cols:]
    side_raw = jnp.einsum("bsd,dc->bsc", normed, w_side, preferred_element_type=jnp.float32)
    halo = from_behind(mixed_raw[:, seg_len - halo_rows :], "ctx", 1)
    raw_ext = jnp.concatenate([halo, mixed_raw], 1).astype(jnp.float32)
    conv_all = jnp.concatenate([conv_q, conv_k, conv_v], 1).astype(jnp.float32)

    def prepare(raw_cols, side_cols, conv_weight, log_rate, rate_bias):
        summed = raw_cols[:, 0:seg_len] * conv_weight[0] * tap_masks[0]
        for offset in range(1, conv_width):
            summed = (
                summed
                + raw_cols[:, offset : offset + seg_len] * conv_weight[offset] * tap_masks[offset]
            )
        active = jax.nn.silu(summed)
        queries = active[..., :key_cols].reshape(streams, seg_len, head_count, key_dim)
        key_rows = active[..., key_cols : 2 * key_cols].reshape(
            streams, seg_len, head_count, key_dim
        )
        values = active[..., 2 * key_cols :].reshape(streams, seg_len, head_count, val_dim)
        queries = (
            queries
            * lax.rsqrt(jnp.sum(queries * queries, -1, keepdims=True) + unit_epsilon)
            * key_dim ** (-0.5)
        )
        key_rows = key_rows * lax.rsqrt(
            jnp.sum(key_rows * key_rows, -1, keepdims=True) + unit_epsilon
        )
        log_decay = -jnp.exp(log_rate) * jax.nn.softplus(side_cols[..., :head_count] + rate_bias)
        beta_gate = jax.nn.sigmoid(side_cols[..., head_count:])
        return (queries, key_rows, values, log_decay, beta_gate)

    prepared, pull_prepare = jax.vjp(prepare, raw_ext, side_raw, conv_all, a_log, dt_bias)
    maps, pull_maps = jax.vjp(partial(block_maps, resets=resets), *prepared)
    moved, added, reader, offset = maps
    before, last = run_blocks(
        moved, added, "bhij,bhjk->bhik", range(seg_len // BLOCK)
    )
    state_in = state_entering(last, val_dim, "ctx")
    states = before[:, :, :, :val_dim] + mm(
        "bhvd,nbhde->nbhve", state_in, before[:, :, :, val_dim:]
    )
    direct = arrange_back(offset + mm("nbhtd,nbhvd->nbhtv", reader, states))
    gated_f, pull_finish = jax.vjp(finish, direct, gate_raw, gain_out_f)
    gated = gated_f.astype(jnp.bfloat16)
    middle = tokens_f + summed_product(gated, w_o, "sc,dc->sd").astype(jnp.float32)
    normed_full, pull_second = jax.vjp(norm_gain, middle, gain_ffn_f)
    normed_ffn = normed_full.astype(jnp.bfloat16)
    paired = jnp.einsum("bsd,dc->bsc", normed_ffn, w_pair, preferred_element_type=jnp.float32)
    gate_val = paired[..., :hidden_cols]
    up_val = paired[..., hidden_cols:]
    hidden = (jax.nn.silu(gate_val) * up_val).astype(jnp.bfloat16)
    layer_out = (middle + summed_product(hidden, w_back, "sf,df->sd").astype(jnp.float32)).astype(
        jnp.bfloat16
    )
    cotangent = d_out.astype(jnp.float32)
    d_hidden = jnp.einsum("bsd,df->bsf", d_out, w_back, preferred_element_type=jnp.float32)
    grad_down = jnp.einsum("bsd,bsf->df", d_out, hidden, preferred_element_type=jnp.float32)
    sig_gate = jax.nn.sigmoid(gate_val)
    d_gate = (d_hidden * up_val * sig_gate * (1.0 + gate_val * (1.0 - sig_gate))).astype(
        jnp.bfloat16
    )
    d_up = (d_hidden * gate_val * sig_gate).astype(jnp.bfloat16)
    d_paired = jnp.concatenate([d_gate, d_up], -1)
    grad_pair = jnp.einsum("bsd,bsc->dc", normed_ffn, d_paired, preferred_element_type=jnp.float32)
    d_normed_ffn = summed_product(d_paired, w_pair, "sc,dc->sd").astype(jnp.float32)
    d_middle_norm, grad_gain_ffn = pull_second(d_normed_ffn)
    d_middle = cotangent + d_middle_norm
    d_attention = d_middle.astype(jnp.bfloat16)
    grad_out_proj = jnp.einsum(
        "bsd,bsc->dc", d_attention, gated, preferred_element_type=jnp.float32
    )
    d_gated = jnp.einsum(
        "bsd,dc->bsc", d_attention, w_o, preferred_element_type=jnp.float32
    )
    early_pack = jnp.concatenate(
        [grad_out_proj, grad_pair, grad_down, grad_gain_ffn[:, None]], 1
    ).astype(jnp.bfloat16)
    early = lax.psum_scatter(early_pack, shards, scatter_dimension=0, tiled=True).astype(
        jnp.float32
    )
    d_direct, d_gate_raw, grad_gain_out = pull_finish(d_gated)
    d_offset = arrange(d_direct)
    d_states = mm("nbhtv,nbhtd->nbhvd", d_offset, reader)
    after, first = run_blocks(
        moved, d_states, "bhij,bhkj->bhik", range(seg_len // BLOCK - 1, -1, -1)
    )
    d_state_out = gradient_entering(first, val_dim, "ctx")
    d_added = after[:, :, :, :val_dim] + mm(
        "bhvd,nbhde->nbhve", d_state_out, after[:, :, :, val_dim:]
    )
    d_moved = mm("nbhvd,nbhve->nbhde", states, d_added)
    d_reader = mm("nbhtv,nbhvd->nbhtd", d_offset, states)
    d_prepared = pull_maps((d_moved, d_added, d_reader, d_offset))
    d_raw_ext, d_side, d_conv, d_log_rate, d_rate_bias = pull_prepare(d_prepared)
    returned = from_behind(d_raw_ext[:, :halo_rows], "ctx", -1)
    d_raw = d_raw_ext[:, halo_rows:]
    d_raw = jnp.concatenate(
        [d_raw[:, : seg_len - halo_rows], d_raw[:, seg_len - halo_rows :] + returned], 1
    )
    d_projected = jnp.concatenate([d_raw, d_gate_raw], -1).astype(jnp.bfloat16)
    d_side_low = d_side.astype(jnp.bfloat16)
    grad_main = jnp.einsum("bsd,bsc->dc", normed, d_projected, preferred_element_type=jnp.float32)
    grad_side = jnp.einsum("bsd,bsc->dc", normed, d_side_low, preferred_element_type=jnp.float32)
    late_pack = jnp.concatenate([grad_main, grad_side], 1).astype(jnp.bfloat16)
    late = lax.psum_scatter(late_pack, shards, scatter_dimension=0, tiled=True).astype(jnp.float32)
    d_all = jnp.concatenate([d_projected, d_side_low], -1)
    d_normed = summed_product(
        d_all, w_first[:, : main_cols + side_cols_all], "sc,dc->sd"
    ).astype(jnp.float32)
    recomputed, pull_first = jax.vjp(norm_gain, tokens_f, gain_attn_f)
    d_tokens_norm, grad_gain_attn = pull_first(d_normed)
    grad_tokens = d_middle + d_tokens_norm
    grad_gain_out = lax.psum(grad_gain_out, "tp")
    pieces = (d_conv, d_log_rate, d_rate_bias, grad_gain_attn, grad_gain_out)
    flat = lax.psum(jnp.concatenate([piece.reshape(-1) for piece in pieces]), shards)
    sums, place = ([], 0)
    for piece in pieces:
        sums.append(flat[place : place + piece.size].reshape(piece.shape))
        place += piece.size
    shard = lax.axis_index(shards)
    own_attn = lax.dynamic_slice_in_dim(sums[3], shard * shard_rows, shard_rows)
    own_out = lax.dynamic_slice_in_dim(sums[4], shard * gain_rows, gain_rows)
    pair_end = val_cols + 2 * hidden_cols
    down_end = pair_end + hidden_cols
    return (
        layer_out,
        grad_tokens,
        late[:, :key_cols],
        late[:, key_cols : 2 * key_cols],
        late[:, 2 * key_cols : mixed_cols],
        late[:, mixed_cols:main_cols],
        late[:, main_cols : main_cols + head_count],
        late[:, main_cols + head_count :],
        early[:, :val_cols],
        early[:, val_cols : val_cols + hidden_cols],
        early[:, val_cols + hidden_cols : pair_end],
        early[:, pair_end:down_end],
        own_attn,
        early[:, down_end],
        own_out,
        sums[0][:, :key_cols],
        sums[0][:, key_cols : 2 * key_cols],
        sums[0][:, 2 * key_cols :],
        sums[1],
        sums[2],
    )


def solution(mesh):
    return jax.shard_map(
        on_device,
        mesh=mesh,
        in_specs=(
            P("dp", "ctx", None),
            P("dp", None),
            P(("dp", "ctx"), "tp"),
            P(("dp", "ctx"), "tp"),
            P(("dp", "ctx"), "tp"),
            P(("dp", "ctx"), "tp"),
            P(("dp", "ctx"), "tp"),
            P(("dp", "ctx"), "tp"),
            P(("dp", "ctx"), "tp"),
            P(("dp", "ctx"), "tp"),
            P(("dp", "ctx"), "tp"),
            P(("dp", "ctx"), "tp"),
            P(("dp", "ctx")),
            P(("dp", "ctx")),
            P(("dp", "ctx")),
            P(None, "tp"),
            P(None, "tp"),
            P(None, "tp"),
            P("tp"),
            P("tp"),
            P("dp", "ctx", None),
        ),
        out_specs=(
            P("dp", "ctx", None),
            P("dp", "ctx", None),
            P(("dp", "ctx"), "tp"),
            P(("dp", "ctx"), "tp"),
            P(("dp", "ctx"), "tp"),
            P(("dp", "ctx"), "tp"),
            P(("dp", "ctx"), "tp"),
            P(("dp", "ctx"), "tp"),
            P(("dp", "ctx"), "tp"),
            P(("dp", "ctx"), "tp"),
            P(("dp", "ctx"), "tp"),
            P(("dp", "ctx"), "tp"),
            P(("dp", "ctx")),
            P(("dp", "ctx")),
            P(("dp", "ctx")),
            P(None, "tp"),
            P(None, "tp"),
            P(None, "tp"),
            P("tp"),
            P("tp"),
        ),
        check_vma=False,
    )
```
